32 devices in a mesh: pole: 2 (over y), prow: 8 (over z, x), pcol: 2 (over core).
Axes of the slice: x: 2, y: 2, z: 4, core: 2. Of those that a mesh axis runs over, the one named last changes fastest.
Arguments:
- inverse_block: bfloat16 [32768, 16384], P(('pole', 'prow'), 'pcol'), parts along dimension 0, may hold values from -0.046875 to 0.046875
- factor_rows: bfloat16 [4, 384, 16384], P('pole', 'prow', 'pcol'), parts along dimension 0, may hold values from -1.5 to 1.5
- pivot_inverse: float32 [4, 384, 384], P('pole', 'prow', 'pcol'), parts along dimension 0, may hold values from -6 to 6
- structure: int32 [2, 128], replicated, may hold values 0 or 1
- block_owner: int32 [128], replicated, may hold values from 0 to 127, each once
Outputs:
- offdiag: bfloat16 [4, 16384, 384], P('pole', 'prow', 'pcol'), parts along dimension 0
- diag_block: float32 [4, 384, 384], P('pole', 'prow', 'pcol'), parts along dimension 0
The draws below stay inside these ranges and needn't reach their ends.
There are 2 independent parts, one for each index of `pole`. The reference program is written for one: setup_inputs(seed, part) draws one part's arguments, and reference() takes and returns one part's arrays. A program takes and returns all parts, laid end to end along the dimension named above; an argument that names none is the same for every part. Nothing has to cross between parts.
All inputs are finite; a program needn't handle non-finite values.
Results may differ from the reference program's by a relative error of at most 0.0021.
Values may be sent and summed in bfloat16 or wider, within the bound.
A program may use at most 128 MiB of HBM per device.

```python
import jax
import jax.numpy as jnp

ANC = 16384
W = 384
NB = 128


def plant(result, own_key, smallest, high):
    extent = result.shape
    index_at = [jax.random.randint(jax.random.fold_in(own_key, axis), (), 0, extent[axis]) for axis in range(len(extent))]
    result = result.at[tuple(index_at)].set(smallest)
    longest = extent.index(max(extent))
    index_at[longest] = (index_at[longest] + 1) % extent[longest]
    return result.at[tuple(index_at)].set(high)


def level_of(rng, dims, shards, low, high):
    level, own = 1.0, jax.random.fold_in(rng, 6)
    for dim, parts in shards:
        heights = jnp.exp(jax.random.uniform(jax.random.fold_in(own, dim), (parts,), jnp.float32, low / len(shards), high / len(shards)))
        level = level * jnp.repeat(heights, dims[dim] // parts).reshape([-1 if axis == dim else 1 for axis in range(len(dims))])
    return level


def centred(key, extent, width, bound, shards=(), dtype=jnp.bfloat16):
    values = width * jax.random.normal(key, extent, jnp.float32)
    if shards:
        values = values * level_of(key, extent, shards, -0.22, 0.18)
    return jnp.clip(values, -bound, bound).astype(dtype)


def setup_inputs(seed: int = 0, part: int = 0) -> dict:
    seeds = jax.random.split(jax.random.key(seed), 6)
    part_keys = jax.random.split(jax.random.fold_in(seeds[5], part), 6)
    inverse_block = centred(part_keys[0], (ANC, ANC), ANC ** -0.5, 0.046875, ((0, 8), (1, 2)))
    factor_rows = centred(part_keys[1], (2, W, ANC), 0.25, 1.5, ((1, 8), (2, 2)))
    pivot_inverse = centred(part_keys[2], (2, W, W), 1.0, 6.0, ((1, 8), (2, 2)), jnp.float32)
    structure = plant((jax.random.randint(seeds[3], (2, NB), 0, 2) < 1).astype(jnp.int32), jax.random.fold_in(seeds[3], 1), 0, 1)
    block_owner = jax.random.permutation(seeds[4], NB).astype(jnp.int32)
    return {"inverse_block": inverse_block, "factor_rows": factor_rows, "pivot_inverse": pivot_inverse, "structure": structure, "block_owner": block_owner}


def reference(inverse_block, factor_rows, pivot_inverse, structure, block_owner):
    active = structure[:, block_owner].astype(jnp.float32)
    cell_mask = jnp.repeat(active, ANC // NB, axis=1)
    outs_off = []
    outs_diag = []
    for supernode in range(2):
        masked = factor_rows[supernode] * cell_mask[supernode][None, :].astype(jnp.bfloat16)
        product = jnp.dot(inverse_block, masked.T, preferred_element_type=jnp.float32)
        offdiag = (-product * cell_mask[supernode][:, None]).astype(jnp.bfloat16)
        diag_term = jnp.dot(masked, offdiag, preferred_element_type=jnp.float32)
        outs_off.append(offdiag)
        outs_diag.append(pivot_inverse[supernode] - diag_term)
    return jnp.stack(outs_off), jnp.stack(outs_diag)
```

```python
import functools

import jax
import jax.numpy as jnp
from jax import lax
from jax.experimental import pallas as pl
from jax.experimental.pallas import tpu as pltpu
from jax.sharding import PartitionSpec as P

ANC = 16384
W = 384
BLK = 128
MESH = pl.DeviceIdType.MESH
CAPACITIES = (32, 36, 40, 48)
CHUNK = 4
SKEW = 2


def from_partner(block, axis, distance):
    count = lax.axis_size(axis)
    route = []
    for low in range(count):
        high = low | 1 << distance
        if high != low and high < count:
            route += [(low, high), (high, low)]
    return lax.ppermute(block, axis, route)


def dense_local(inverse_block, factor_rows, pivot_inverse, structure, block_owner):
    rows_dev = inverse_block.shape[0]
    half_cols = inverse_block.shape[1]
    row_index = lax.axis_index("prow")
    col_index = lax.axis_index("pcol")
    grid_rows = lax.axis_size("prow")
    blocks = structure.shape[1]
    position = jnp.arange(blocks, dtype=jnp.int32)
    onehot = (block_owner[:, None] == position[None, :]).astype(jnp.float32)
    active = jnp.dot(structure.astype(jnp.float32), onehot.T, precision=lax.Precision.HIGHEST)
    cell_mask = jnp.repeat(active, ANC // blocks, axis=1)
    half_mask = lax.dynamic_slice_in_dim(cell_mask, col_index * half_cols, half_cols, 1)
    own_mask = lax.dynamic_slice_in_dim(cell_mask, row_index * rows_dev, rows_dev, 1)
    masked = factor_rows * half_mask[:, None, :].astype(jnp.bfloat16)
    holds_block = row_index * rows_dev // half_cols == col_index
    offset = jnp.clip(row_index * rows_dev - col_index * half_cols, 0, half_cols - rows_dev)
    outs_off = []
    outs_diag = []
    diag_rows = W // grid_rows
    for supernode in range(2):
        segment = lax.all_gather(masked[supernode], "prow", axis=0, tiled=True)
        running = lax.dot_general(
            inverse_block, segment, (((1,), (1,)), ((), ())), preferred_element_type=jnp.float32
        )
        own_cols = lax.dynamic_slice_in_dim(segment, offset, rows_dev, 1)
        own_cols = jnp.where(holds_block, own_cols, jnp.zeros_like(own_cols))
        shared_part = lax.psum_scatter(running, "pcol", scatter_dimension=1, tiled=True)
        offdiag = (-shared_part * own_mask[supernode][:, None]).astype(jnp.bfloat16)
        partner = from_partner(own_cols, "pcol", 0)
        own_factor = jnp.where(holds_block, own_cols, partner)
        diag_term = jnp.dot(own_factor, offdiag, preferred_element_type=jnp.float32)
        summed = lax.psum(diag_term, "prow")
        own_rows_sum = lax.dynamic_slice_in_dim(summed, row_index * diag_rows, diag_rows, 0)
        outs_off.append(offdiag)
        outs_diag.append(pivot_inverse[supernode] - own_rows_sum)
    return (jnp.stack(outs_off), jnp.stack(outs_diag))


def list_kernel(blocks, half_blocks, structure, owner, slots, valid, place, act, counts):
    def clear(i, carry):
        slots[i] = 0
        valid[i] = 0
        return carry

    lax.fori_loop(0, 2 * blocks, clear, 0, unroll=8)

    def step(s, found):
        found = list(found)
        for half in range(2):
            logical = owner[half * half_blocks + s]
            for k in range(2):
                lane = half * 2 + k
                a = structure[k, logical]
                n = found[lane]
                slots[lane * half_blocks + n] = s * a
                valid[lane * half_blocks + n] = a
                place[k * blocks + half * half_blocks + s] = n * a
                act[k * blocks + half * half_blocks + s] = a
                found[lane] = n + a
        return tuple(found)

    zero = jnp.int32(0)
    found = lax.fori_loop(0, half_blocks, step, (zero,) * 4, unroll=4)
    for lane in range(4):
        counts[lane] = found[lane]


def gather_kernel(
    cap, m, n, slots, valid, place, act, inv_hbm, factor, pivot, off, diag,
    inv, panels, g0, g1, acc, exch, own, dsend, drecv,
    inv_sem, send_sem, recv_sem, ex_sem, own_sem, ds_sem, dr_sem,
):
    r = lax.axis_index("prow")
    q = lax.axis_index("pcol")
    half_blocks, rows_dev, _ = inv.shape
    half_cols = half_blocks * BLK
    blocks = 2 * half_blocks
    row_blocks = rows_dev // BLK
    per_half = n // 2
    fr = factor.shape[1]
    nch = cap // m
    total = 2 * nch
    gathered = (g0, g1)
    z, x = r // 2, r % 2
    p = z + x * (n - 1 - 2 * z)

    def device_at(pos):
        pos = (pos + 2 * n) % n
        u = pos // (n // 2)
        return 2 * pos + u * (2 * n - 1 - 4 * pos)

    right, left = device_at(p + 1), device_at(p - 1)

    def load(s):
        return pltpu.make_async_copy(
            inv_hbm.at[:, pl.ds(pl.multiple_of(s * BLK, BLK), BLK)], inv.at[s], inv_sem.at[s]
        )

    barrier = pltpu.get_barrier_semaphore()
    for d in range(1, n):
        pl.semaphore_signal(
            barrier, inc=1, device_id={"prow": (r + d) % n}, device_id_type=MESH
        )
    pl.semaphore_signal(barrier, inc=1, device_id={"pcol": 1 - q}, device_id_type=MESH)

    def split(s, carry):
        for k in range(2):
            panels[k, s] = factor[k, :, pl.ds(pl.multiple_of(s * BLK, BLK), BLK)]
        return carry

    lax.fori_loop(0, half_blocks, split, 0, unroll=4)

    for k in range(2):
        base = (q * 2 + k) * half_blocks

        def pack(j, carry, k=k, base=base):
            for i in range(m):
                slot = j * m + i
                panel = panels[k, slots[base + slot]].astype(jnp.float32)
                panel = panel * valid[base + slot].astype(jnp.float32)
                gathered[k][slot, r] = panel.astype(jnp.bfloat16)
            return carry

        lax.fori_loop(0, nch, pack, 0)

    pl.semaphore_wait(barrier, n)

    def ring(k, j, c, d, t):
        sign = 1 - 2 * d
        src = device_at(p - sign * (t - 1))
        part = pl.ds(j * m, m) if t < n // 2 else pl.ds(j * m + d * (m // 2), m // 2)
        ref = gathered[k].at[part, src]
        return pltpu.make_async_remote_copy(
            src_ref=ref,
            dst_ref=ref,
            send_sem=send_sem.at[d, t - 1, c],
            recv_sem=recv_sem.at[d, t - 1, c],
            device_id={"prow": (right, left)[d]},
            device_id_type=MESH,
        )

    def landed(k, j, c, d, t):
        sign = 1 - 2 * d
        src = device_at(p - sign * t)
        part = pl.ds(j * m, m) if t < n // 2 else pl.ds(j * m + d * (m // 2), m // 2)
        ref = gathered[k].at[part, src]
        pltpu.make_async_remote_copy(
            src_ref=ref,
            dst_ref=ref,
            send_sem=send_sem.at[d, t - 1, c],
            recv_sem=recv_sem.at[d, t - 1, c],
            device_id={"prow": (right, left)[d]},
            device_id_type=MESH,
        ).wait_recv()

    def on_chunk(c, do):
        for k in range(2):
            pl.when((c >= k * nch) & (c < (k + 1) * nch))(
                functools.partial(do, k, c - k * nch, c)
            )

    hops = n // 2

    def hop(t, k, j, c):
        for d in range(2):
            if t > 1:
                landed(k, j, c, d, t - 1)
            ring(k, j, c, d, t).start()

    tile = 512

    def product(k, j, c):
        base = (q * 2 + k) * half_blocks + j * m
        cols = [slots[base + i] for i in range(m)]

        def rows_step(i, carry):
            rows = pl.ds(pl.multiple_of(i * tile, tile), tile)
            lhs = jnp.concatenate([inv[s, rows, :] for s in cols], axis=1)
            for h in range(2):
                rhs = jnp.concatenate(
                    [
                        gathered[k][j * m + i, h * per_half:(h + 1) * per_half].reshape(
                            per_half * fr, BLK
                        )
                        for i in range(m)
                    ],
                    axis=1,
                )
                part = lax.dot_general(
                    lhs, rhs, (((1,), (1,)), ((), ())), preferred_element_type=jnp.float32
                )
                before = acc[h, rows, :]
                acc[h, rows, :] = jnp.where(j == 0, 0.0, before) + part
            return carry

        lax.fori_loop(0, rows_dev // tile, rows_step, 0)

    def exchange(k):
        return pltpu.make_async_remote_copy(
            src_ref=acc.at[1 - q],
            dst_ref=exch.at[k],
            send_sem=ex_sem.at[k, 0],
            recv_sem=ex_sem.at[k, 1],
            device_id={"pcol": 1 - q},
            device_id_type=MESH,
        )

    def hand_over(k):
        return pltpu.make_async_remote_copy(
            src_ref=own.at[k],
            dst_ref=own.at[k],
            send_sem=own_sem.at[k, 0],
            recv_sem=own_sem.at[k, 1],
            device_id={"pcol": 1 - q},
            device_id_type=MESH,
        )

    holds = r * rows_dev // half_cols == q

    def begin_exchange(k):
        exchange(k).start()

        @pl.when(holds)
        def _():
            for b in range(row_blocks):
                at = k * blocks + r * row_blocks + b
                own[k, :, :, b * BLK:(b + 1) * BLK] = gathered[k][place[at]]
            hand_over(k).start()

    def diag_send(k, d):
        to = (r + d) % n
        return pltpu.make_async_remote_copy(
            src_ref=dsend.at[k, to],
            dst_ref=drecv.at[k, n - d],
            send_sem=ds_sem.at[k, d],
            recv_sem=dr_sem.at[k, n - d],
            device_id={"prow": to},
            device_id_type=MESH,
        )

    def finish_exchange(k):
        exchange(k).wait()
        for b in range(row_blocks):
            rows = slice(b * BLK, (b + 1) * BLK)
            mask = act[k * blocks + r * row_blocks + b].astype(jnp.float32)
            shared = acc[q, rows, :] + exch[k, rows, :]
            off[k, rows, :] = (-shared * mask).astype(jnp.bfloat16)

        @pl.when(holds)
        def _():
            hand_over(k).wait_send()

        @pl.when(jnp.logical_not(holds))
        def _():
            hand_over(k).wait_recv()

        term = jnp.dot(
            own[k].reshape(n * fr, rows_dev), off[k], preferred_element_type=jnp.float32
        )
        dsend[k] = term.reshape(n, fr, term.shape[1])
        for d in range(1, n):
            diag_send(k, d).start()

    def compute(k, j, c):
        for d in range(2):
            landed(k, j, c, d, hops)
        if k == 1:
            pl.when(j == 0)(functools.partial(finish_exchange, 0))
        else:
            @pl.when(j == 0)
            def _():
                lax.fori_loop(0, half_blocks, lambda s, x: (load(s).wait(), x)[1], 0)

        product(k, j, c)
        pl.when(j == nch - 1)(functools.partial(begin_exchange, k))

    lax.fori_loop(0, half_blocks, lambda s, x: (load(s).start(), x)[1], 0)

    def tick(tau, carry):
        for t in range(hops, 0, -1):
            on_chunk(tau - SKEW * (t - 1), functools.partial(hop, t))
        on_chunk(tau - SKEW * (hops - 1) - 1, compute)
        return carry

    lax.fori_loop(0, total + SKEW * (hops - 1) + 1, tick, 0)
    finish_exchange(1)

    def drain(c, carry):
        def one(k, j, c):
            for d in range(2):
                for t in range(1, hops + 1):
                    ring(k, j, c, d, t).wait_send()

        on_chunk(c, one)
        return carry

    lax.fori_loop(0, total, drain, 0)

    for k in range(2):
        summed = dsend[k, r]
        for d in range(1, n):
            diag_send(k, n - d).wait_recv()
            summed = summed + drecv[k, d]
        diag[k] = pivot[k] - summed
    for k in range(2):
        for d in range(1, n):
            diag_send(k, d).wait_send()


def gathered_local(index, cap, m, lists, inverse_block, factor_rows, pivot_inverse):
    n = lax.axis_size("prow")
    rows_dev, half_cols = inverse_block.shape
    fr = factor_rows.shape[1]
    half_w = pivot_inverse.shape[2]
    nch = cap // m
    smem = pl.BlockSpec(memory_space=pltpu.SMEM)
    vmem = pl.BlockSpec(memory_space=pltpu.VMEM)
    hops = n // 2
    return pl.pallas_call(
        functools.partial(gather_kernel, cap, m, n),
        out_shape=(
            jax.ShapeDtypeStruct((2, rows_dev, half_w), jnp.bfloat16),
            jax.ShapeDtypeStruct((2, fr, half_w), jnp.float32),
        ),
        in_specs=[smem] * 4 + [pl.BlockSpec(memory_space=pl.ANY), vmem, vmem],
        out_specs=(vmem, vmem),
        scratch_shapes=[
            pltpu.VMEM((half_cols // BLK, rows_dev, BLK), jnp.bfloat16),
            pltpu.VMEM((2, half_cols // BLK, fr, BLK), jnp.bfloat16),
            pltpu.VMEM((cap, n, fr, BLK), jnp.bfloat16),
            pltpu.VMEM((cap, n, fr, BLK), jnp.bfloat16),
            pltpu.VMEM((2, rows_dev, half_w), jnp.float32),
            pltpu.VMEM((2, rows_dev, half_w), jnp.float32),
            pltpu.VMEM((2, n, fr, rows_dev), jnp.bfloat16),
            pltpu.VMEM((2, n, fr, half_w), jnp.float32),
            pltpu.VMEM((2, n, fr, half_w), jnp.float32),
            pltpu.SemaphoreType.DMA((half_cols // BLK,)),
            pltpu.SemaphoreType.DMA((2, hops, 2 * nch)),
            pltpu.SemaphoreType.DMA((2, hops, 2 * nch)),
            pltpu.SemaphoreType.DMA((2, 2)),
            pltpu.SemaphoreType.DMA((2, 2)),
            pltpu.SemaphoreType.DMA((2, n)),
            pltpu.SemaphoreType.DMA((2, n)),
        ],
        compiler_params=pltpu.CompilerParams(
            collective_id=index, has_side_effects=True, vmem_limit_bytes=63 * 1024 * 1024
        ),
        name=f"gather_{cap}",
    )(*lists, inverse_block, factor_rows, pivot_inverse)


def local(inverse_block, factor_rows, pivot_inverse, structure, block_owner):
    n = lax.axis_size("prow")
    rows_dev, half_cols = inverse_block.shape
    blocks = structure.shape[1]
    fits = (
        n == 8
        and factor_rows.shape[1] % 16 == 0
        and half_cols == blocks // 2 * BLK
        and rows_dev % 512 == 0
    )
    if not fits:
        return dense_local(inverse_block, factor_rows, pivot_inverse, structure, block_owner)
    smem = pl.BlockSpec(memory_space=pltpu.SMEM)
    *lists, counts = pl.pallas_call(
        functools.partial(list_kernel, blocks, blocks // 2),
        out_shape=(
            *[jax.ShapeDtypeStruct((2 * blocks,), jnp.int32)] * 4,
            jax.ShapeDtypeStruct((4,), jnp.int32),
        ),
        in_specs=[smem, smem],
        out_specs=(smem,) * 5,
        name="block_lists",
    )(structure, block_owner)
    most = jnp.max(counts)
    choice = sum((most > cap).astype(jnp.int32) for cap in CAPACITIES)

    def gathering(index, cap):
        def run(inv, factor, pivot, structure, owner, *lists):
            return gathered_local(index, cap, CHUNK, lists, inv, factor, pivot)

        return run

    def whole(inv, factor, pivot, structure, owner, *lists):
        return dense_local(inv, factor, pivot, structure, owner)

    branches = [gathering(index, cap) for index, cap in enumerate(CAPACITIES)] + [whole]
    return lax.switch(
        choice, branches, inverse_block, factor_rows, pivot_inverse, structure, block_owner, *lists
    )


def solution(mesh):
    return jax.shard_map(
        local,
        mesh=mesh,
        in_specs=(
            P(("pole", "prow"), "pcol"),
            P("pole", "prow", "pcol"),
            P("pole", "prow", "pcol"),
            P(),
            P(),
        ),
        out_specs=(P("pole", "prow", "pcol"), P("pole", "prow", "pcol")),
        check_vma=False,
    )
```

```python
import functools

import jax
import jax.numpy as jnp
from jax import lax
from jax.experimental import pallas as pl
from jax.experimental.pallas import tpu as pltpu
from jax.sharding import PartitionSpec as P

ANC = 16384
W = 384
BLK = 128
MESH = pl.DeviceIdType.MESH
CAPACITIES = (36, 40, 48)
CHUNK = 4
SKEW = 2


def from_partner(block, axis, distance):
    count = lax.axis_size(axis)
    route = []
    for low in range(count):
        high = low | 1 << distance
        if high != low and high < count:
            route += [(low, high), (high, low)]
    return lax.ppermute(block, axis, route)


def dense_local(inverse_block, factor_rows, pivot_inverse, structure, block_owner):
    rows_dev = inverse_block.shape[0]
    half_cols = inverse_block.shape[1]
    row_index = lax.axis_index("prow")
    col_index = lax.axis_index("pcol")
    grid_rows = lax.axis_size("prow")
    blocks = structure.shape[1]
    position = jnp.arange(blocks, dtype=jnp.int32)
    onehot = (block_owner[:, None] == position[None, :]).astype(jnp.float32)
    active = jnp.dot(structure.astype(jnp.float32), onehot.T, precision=lax.Precision.HIGHEST)
    cell_mask = jnp.repeat(active, ANC // blocks, axis=1)
    half_mask = lax.dynamic_slice_in_dim(cell_mask, col_index * half_cols, half_cols, 1)
    own_mask = lax.dynamic_slice_in_dim(cell_mask, row_index * rows_dev, rows_dev, 1)
    masked = factor_rows * half_mask[:, None, :].astype(jnp.bfloat16)
    holds_block = row_index * rows_dev // half_cols == col_index
    offset = jnp.clip(row_index * rows_dev - col_index * half_cols, 0, half_cols - rows_dev)
    outs_off = []
    outs_diag = []
    diag_rows = W // grid_rows
    for supernode in range(2):
        segment = lax.all_gather(masked[supernode], "prow", axis=0, tiled=True)
        running = lax.dot_general(
            inverse_block, segment, (((1,), (1,)), ((), ())), preferred_element_type=jnp.float32
        )
        own_cols = lax.dynamic_slice_in_dim(segment, offset, rows_dev, 1)
        own_cols = jnp.where(holds_block, own_cols, jnp.zeros_like(own_cols))
        shared_part = lax.psum_scatter(running, "pcol", scatter_dimension=1, tiled=True)
        offdiag = (-shared_part * own_mask[supernode][:, None]).astype(jnp.bfloat16)
        partner = from_partner(own_cols, "pcol", 0)
        own_factor = jnp.where(holds_block, own_cols, partner)
        diag_term = jnp.dot(own_factor, offdiag, preferred_element_type=jnp.float32)
        summed = lax.psum(diag_term, "prow")
        own_rows_sum = lax.dynamic_slice_in_dim(summed, row_index * diag_rows, diag_rows, 0)
        outs_off.append(offdiag)
        outs_diag.append(pivot_inverse[supernode] - own_rows_sum)
    return (jnp.stack(outs_off), jnp.stack(outs_diag))


def list_kernel(blocks, half_blocks, structure, owner, slots, valid, place, act, counts):
    def clear(i, carry):
        slots[i] = 0
        valid[i] = 0
        return carry

    lax.fori_loop(0, 2 * blocks, clear, 0, unroll=8)

    def step(s, found):
        found = list(found)
        for half in range(2):
            logical = owner[half * half_blocks + s]
            for k in range(2):
                lane = half * 2 + k
                a = structure[k, logical]
                n = found[lane]
                slots[lane * half_blocks + n] = s * a
                valid[lane * half_blocks + n] = a
                place[k * blocks + half * half_blocks + s] = n * a
                act[k * blocks + half * half_blocks + s] = a
                found[lane] = n + a
        return tuple(found)

    zero = jnp.int32(0)
    found = lax.fori_loop(0, half_blocks, step, (zero,) * 4, unroll=4)
    for lane in range(4):
        counts[lane] = found[lane]


def gather_kernel(
    cap, m, n, slots, valid, place, act, inv_hbm, factor, pivot, off, diag,
    inv, panels, g0, g1, acc, exch, own, dsend, drecv,
    inv_sem, send_sem, recv_sem, ex_sem, own_sem, ds_sem, dr_sem,
):
    r = lax.axis_index("prow")
    q = lax.axis_index("pcol")
    half_blocks, rows_dev, _ = inv.shape
    half_cols = half_blocks * BLK
    blocks = 2 * half_blocks
    row_blocks = rows_dev // BLK
    per_half = n // 2
    fr = factor.shape[1]
    nch = cap // m
    total = 2 * nch
    gathered = (g0, g1)
    z, x = r // 2, r % 2
    p = z + x * (n - 1 - 2 * z)

    def device_at(pos):
        pos = (pos + 2 * n) % n
        u = pos // (n // 2)
        return 2 * pos + u * (2 * n - 1 - 4 * pos)

    right, left = device_at(p + 1), device_at(p - 1)

    def load(s):
        return pltpu.make_async_copy(
            inv_hbm.at[:, pl.ds(pl.multiple_of(s * BLK, BLK), BLK)], inv.at[s], inv_sem.at[s]
        )

    lax.fori_loop(0, half_blocks, lambda s, x: (load(s).start(), x)[1], 0)

    barrier = pltpu.get_barrier_semaphore()
    for d in range(1, n):
        pl.semaphore_signal(
            barrier, inc=1, device_id={"prow": (r + d) % n}, device_id_type=MESH
        )
    pl.semaphore_signal(barrier, inc=1, device_id={"pcol": 1 - q}, device_id_type=MESH)

    def split(s, carry):
        for k in range(2):
            panels[k, s] = factor[k, :, pl.ds(pl.multiple_of(s * BLK, BLK), BLK)]
        return carry

    lax.fori_loop(0, half_blocks, split, 0, unroll=4)

    for k in range(2):
        base = (q * 2 + k) * half_blocks

        def pack(j, carry, k=k, base=base):
            for i in range(m):
                slot = j * m + i
                panel = panels[k, slots[base + slot]].astype(jnp.float32)
                panel = panel * valid[base + slot].astype(jnp.float32)
                gathered[k][slot, r] = panel.astype(jnp.bfloat16)
            return carry

        lax.fori_loop(0, nch, pack, 0)

    pl.semaphore_wait(barrier, n)

    def ring(k, j, c, d, t):
        sign = 1 - 2 * d
        src = device_at(p - sign * (t - 1))
        part = pl.ds(j * m, m) if t < n // 2 else pl.ds(j * m + d * (m // 2), m // 2)
        ref = gathered[k].at[part, src]
        return pltpu.make_async_remote_copy(
            src_ref=ref,
            dst_ref=ref,
            send_sem=send_sem.at[d, t - 1, c],
            recv_sem=recv_sem.at[d, t - 1, c],
            device_id={"prow": (right, left)[d]},
            device_id_type=MESH,
        )

    def landed(k, j, c, d, t):
        sign = 1 - 2 * d
        src = device_at(p - sign * t)
        part = pl.ds(j * m, m) if t < n // 2 else pl.ds(j * m + d * (m // 2), m // 2)
        ref = gathered[k].at[part, src]
        pltpu.make_async_remote_copy(
            src_ref=ref,
            dst_ref=ref,
            send_sem=send_sem.at[d, t - 1, c],
            recv_sem=recv_sem.at[d, t - 1, c],
            device_id={"prow": (right, left)[d]},
            device_id_type=MESH,
        ).wait_recv()

    def on_chunk(c, do):
        for k in range(2):
            pl.when((c >= k * nch) & (c < (k + 1) * nch))(
                functools.partial(do, k, c - k * nch, c)
            )

    hops = n // 2

    def hop(t, k, j, c):
        for d in range(2):
            if t > 1:
                landed(k, j, c, d, t - 1)
            ring(k, j, c, d, t).start()

    tile = 512

    def product(k, j, c):
        base = (q * 2 + k) * half_blocks + j * m
        cols = [slots[base + i] for i in range(m)]

        def rows_step(i, carry):
            rows = pl.ds(pl.multiple_of(i * tile, tile), tile)
            lhs = jnp.concatenate([inv[s, rows, :] for s in cols], axis=1)
            for h in range(2):
                rhs = jnp.concatenate(
                    [
                        gathered[k][j * m + i, h * per_half:(h + 1) * per_half].reshape(
                            per_half * fr, BLK
                        )
                        for i in range(m)
                    ],
                    axis=1,
                )
                part = lax.dot_general(
                    lhs, rhs, (((1,), (1,)), ((), ())), preferred_element_type=jnp.float32
                )
                before = acc[h, rows, :]
                acc[h, rows, :] = jnp.where(j == 0, 0.0, before) + part
            return carry

        lax.fori_loop(0, rows_dev // tile, rows_step, 0)

    def exchange(k):
        return pltpu.make_async_remote_copy(
            src_ref=acc.at[1 - q],
            dst_ref=exch.at[k],
            send_sem=ex_sem.at[k, 0],
            recv_sem=ex_sem.at[k, 1],
            device_id={"pcol": 1 - q},
            device_id_type=MESH,
        )

    def hand_over(k):
        return pltpu.make_async_remote_copy(
            src_ref=own.at[k],
            dst_ref=own.at[k],
            send_sem=own_sem.at[k, 0],
            recv_sem=own_sem.at[k, 1],
            device_id={"pcol": 1 - q},
            device_id_type=MESH,
        )

    holds = r * rows_dev // half_cols == q

    def begin_exchange(k):
        exchange(k).start()

        @pl.when(holds)
        def _():
            for b in range(row_blocks):
                at = k * blocks + r * row_blocks + b
                own[k, :, :, b * BLK:(b + 1) * BLK] = gathered[k][place[at]]
            hand_over(k).start()

    def diag_send(k, d):
        to = (r + d) % n
        return pltpu.make_async_remote_copy(
            src_ref=dsend.at[k, to],
            dst_ref=drecv.at[k, n - d],
            send_sem=ds_sem.at[k, d],
            recv_sem=dr_sem.at[k, n - d],
            device_id={"prow": to},
            device_id_type=MESH,
        )

    def finish_exchange(k):
        exchange(k).wait()
        for b in range(row_blocks):
            rows = slice(b * BLK, (b + 1) * BLK)
            mask = act[k * blocks + r * row_blocks + b].astype(jnp.float32)
            shared = acc[q, rows, :] + exch[k, rows, :]
            off[k, rows, :] = (-shared * mask).astype(jnp.bfloat16)

        @pl.when(holds)
        def _():
            hand_over(k).wait_send()

        @pl.when(jnp.logical_not(holds))
        def _():
            hand_over(k).wait_recv()

        term = jnp.dot(
            own[k].reshape(n * fr, rows_dev), off[k], preferred_element_type=jnp.float32
        )
        dsend[k] = term.reshape(n, fr, term.shape[1])
        for d in range(1, n):
            diag_send(k, d).start()

    def compute(k, j, c):
        for d in range(2):
            landed(k, j, c, d, hops)
        if k == 1:
            pl.when(j == 0)(functools.partial(finish_exchange, 0))
        else:
            @pl.when(j == 0)
            def _():
                lax.fori_loop(0, half_blocks, lambda s, x: (load(s).wait(), x)[1], 0)

        product(k, j, c)
        pl.when(j == nch - 1)(functools.partial(begin_exchange, k))


    def tick(tau, carry):
        for t in (1, *range(hops, 1, -1)):
            on_chunk(tau - SKEW * (t - 1), functools.partial(hop, t))
        on_chunk(tau - SKEW * (hops - 1) - 1, compute)
        return carry

    lax.fori_loop(0, total + SKEW * (hops - 1) + 1, tick, 0)
    finish_exchange(1)

    def drain(c, carry):
        def one(k, j, c):
            for d in range(2):
                for t in range(1, hops + 1):
                    ring(k, j, c, d, t).wait_send()

        on_chunk(c, one)
        return carry

    lax.fori_loop(0, total, drain, 0)

    for k in range(2):
        summed = dsend[k, r]
        for d in range(1, n):
            diag_send(k, n - d).wait_recv()
            summed = summed + drecv[k, d]
        diag[k] = pivot[k] - summed
    for k in range(2):
        for d in range(1, n):
            diag_send(k, d).wait_send()


def gathered_local(index, cap, m, lists, inverse_block, factor_rows, pivot_inverse):
    n = lax.axis_size("prow")
    rows_dev, half_cols = inverse_block.shape
    fr = factor_rows.shape[1]
    half_w = pivot_inverse.shape[2]
    nch = cap // m
    smem = pl.BlockSpec(memory_space=pltpu.SMEM)
    vmem = pl.BlockSpec(memory_space=pltpu.VMEM)
    hops = n // 2
    return pl.pallas_call(
        functools.partial(gather_kernel, cap, m, n),
        out_shape=(
            jax.ShapeDtypeStruct((2, rows_dev, half_w), jnp.bfloat16),
            jax.ShapeDtypeStruct((2, fr, half_w), jnp.float32),
        ),
        in_specs=[smem] * 4 + [pl.BlockSpec(memory_space=pl.ANY), vmem, vmem],
        out_specs=(vmem, vmem),
        scratch_shapes=[
            pltpu.VMEM((half_cols // BLK, rows_dev, BLK), jnp.bfloat16),
            pltpu.VMEM((2, half_cols // BLK, fr, BLK), jnp.bfloat16),
            pltpu.VMEM((cap, n, fr, BLK), jnp.bfloat16),
            pltpu.VMEM((cap, n, fr, BLK), jnp.bfloat16),
            pltpu.VMEM((2, rows_dev, half_w), jnp.float32),
            pltpu.VMEM((2, rows_dev, half_w), jnp.float32),
            pltpu.VMEM((2, n, fr, rows_dev), jnp.bfloat16),
            pltpu.VMEM((2, n, fr, half_w), jnp.float32),
            pltpu.VMEM((2, n, fr, half_w), jnp.float32),
            pltpu.SemaphoreType.DMA((half_cols // BLK,)),
            pltpu.SemaphoreType.DMA((2, hops, 2 * nch)),
            pltpu.SemaphoreType.DMA((2, hops, 2 * nch)),
            pltpu.SemaphoreType.DMA((2, 2)),
            pltpu.SemaphoreType.DMA((2, 2)),
            pltpu.SemaphoreType.DMA((2, n)),
            pltpu.SemaphoreType.DMA((2, n)),
        ],
        compiler_params=pltpu.CompilerParams(
            collective_id=index, has_side_effects=True, vmem_limit_bytes=63 * 1024 * 1024
        ),
        name=f"gather_{cap}",
    )(*lists, inverse_block, factor_rows, pivot_inverse)


def local(inverse_block, factor_rows, pivot_inverse, structure, block_owner):
    n = lax.axis_size("prow")
    rows_dev, half_cols = inverse_block.shape
    blocks = structure.shape[1]
    fits = (
        n == 8
        and factor_rows.shape[1] % 16 == 0
        and half_cols == blocks // 2 * BLK
        and rows_dev % 512 == 0
    )
    if not fits:
        return dense_local(inverse_block, factor_rows, pivot_inverse, structure, block_owner)
    smem = pl.BlockSpec(memory_space=pltpu.SMEM)
    *lists, counts = pl.pallas_call(
        functools.partial(list_kernel, blocks, blocks // 2),
        out_shape=(
            *[jax.ShapeDtypeStruct((2 * blocks,), jnp.int32)] * 4,
            jax.ShapeDtypeStruct((4,), jnp.int32),
        ),
        in_specs=[smem, smem],
        out_specs=(smem,) * 5,
        name="block_lists",
    )(structure, block_owner)
    most = jnp.max(counts)
    choice = sum((most > cap).astype(jnp.int32) for cap in CAPACITIES)

    def gathering(index, cap):
        def run(inv, factor, pivot, structure, owner, *lists):
            return gathered_local(index, cap, CHUNK, lists, inv, factor, pivot)

        return run

    def whole(inv, factor, pivot, structure, owner, *lists):
        return dense_local(inv, factor, pivot, structure, owner)

    branches = [gathering(index, cap) for index, cap in enumerate(CAPACITIES)] + [whole]
    return lax.switch(
        choice, branches, inverse_block, factor_rows, pivot_inverse, structure, block_owner, *lists
    )


def solution(mesh):
    return jax.shard_map(
        local,
        mesh=mesh,
        in_specs=(
            P(("pole", "prow"), "pcol"),
            P("pole", "prow", "pcol"),
            P("pole", "prow", "pcol"),
            P(),
            P(),
        ),
        out_specs=(P("pole", "prow", "pcol"), P("pole", "prow", "pcol")),
        check_vma=False,
    )
```
